512 devices in a mesh: row: 16 (over z), col: 32 (over y, x, core).
Axes of the slice: x: 4, y: 4, z: 16, core: 2. Of those that a mesh axis runs over, the one named last changes fastest.
Arguments:
- x_panel: bfloat16 [8192, 4096], P('col', 'row'), may hold values from -16 to 16
- grad_out: bfloat16 [2, 8192, 10240], P(None, 'row', 'col'), may hold values from -0.1 to 0.1
- row_state: float32 [2, 4096], P(None, 'row'), may hold values from 0 to 163.84, as said below
- col_state: float32 [2, 10240], P(None, 'col'), may hold values from 0 to 163.84, as said below
Outputs:
- direction: float32 [2, 4096, 10240], P(None, 'row', 'col')
- new_rows: float32 [2, 4096], P(None, 'row')
- new_cols: float32 [2, 10240], P(None, 'col')
The draws below stay inside these ranges and needn't reach their ends.
Inputs may be any that keep to these rules, and one draw needn't show every extreme that they name: `row_state`: positive. `col_state`: positive.
All inputs are finite; a program needn't handle non-finite values.
Results may differ from the reference program's by a relative error of at most 0.0003.
Values may be sent and summed in bfloat16 or wider, within the bound.
A program may use at most 64 MiB of HBM per device.

```python
import math
import jax
import jax.numpy as jnp
from jax import lax

D = 4096
FF = 10240
TOKENS = 8192


def ramp_scales(key, width, flip):
    position = jnp.arange(width, dtype=jnp.float32) / width
    ramp = flip + (1.0 - 2.0 * flip) * position
    noise = jax.random.uniform(key, (width,), jnp.float32)
    return jnp.exp(math.log(math.sqrt(10.0)) * (ramp + noise - 1.0))


def spread_scales(key, width, top):
    spread = jax.random.uniform(key, (width,), jnp.float32)
    return top * jnp.exp(-math.log(32.0) * spread)


def token_group(key):
    return jax.random.randint(jax.random.fold_in(key, 15), (TOKENS, 1), 0, 2) == 0


def feature_scales(key):
    first = ramp_scales(jax.random.fold_in(key, 11), D, 0.0)
    second = spread_scales(jax.random.fold_in(key, 12), D, 3.0)
    return (first, second)


def unit_scales(key):
    first = ramp_scales(jax.random.fold_in(key, 13), FF, 1.0)
    second = spread_scales(jax.random.fold_in(key, 14), FF, 5.0)
    return (first, second)


def draw_x_panel(key, part):
    group = token_group(key)
    first, second = feature_scales(key)
    key = jax.random.fold_in(key, 1)
    base = jnp.clip(jax.random.normal(jax.random.fold_in(key, 8), (TOKENS, D), jnp.float32), -5.0, 5.0)
    scales = jnp.where(group, first[None, :], second[None, :])
    return (base * scales).astype(jnp.bfloat16)


def draw_grad_out(key, part):
    group = token_group(key)
    first, second = unit_scales(key)
    key = jax.random.fold_in(key, 2)
    base = jnp.clip(jax.random.normal(jax.random.fold_in(key, 8), (2, TOKENS, FF), jnp.float32), -5.0, 5.0)
    scales = jnp.where(group[None, :, :], first[None, None, :], second[None, None, :])
    return (0.0039 * base * scales).astype(jnp.bfloat16)


def draw_row_state(key, part):
    first, second = feature_scales(key)
    key = jax.random.fold_in(key, 3)
    low_end = math.log(0.1)
    high_end = math.log(10.0)
    ramp = jnp.arange(D, dtype=jnp.float32) / D
    noise = jax.random.uniform(key, (2, D), jnp.float32, -0.3, 0.3)
    factor = jnp.exp(low_end + (high_end - low_end) * ramp[None, :] + noise)
    level = 1.2 * first * first + 2.9 * second * second
    return TOKENS * 1e-05 * level[None, :] * factor


def draw_col_state(key, part):
    first, second = unit_scales(key)
    key = jax.random.fold_in(key, 4)
    heavy = jax.random.randint(jax.random.fold_in(key, 5), (), 0, 2)
    light_factor = jnp.exp(jax.random.uniform(jax.random.fold_in(key, 6), (2, FF), jnp.float32, math.log(0.05), math.log(0.5)))
    heavy_factor = jnp.exp(jax.random.uniform(jax.random.fold_in(key, 7), (2, FF), jnp.float32, math.log(8.0), math.log(48.0)))
    chosen = jnp.arange(2, dtype=jnp.int32)[:, None] == heavy
    factor = jnp.where(chosen, heavy_factor, light_factor)
    level = first * first + second * second
    return TOKENS * 1.1e-05 * level[None, :] * factor


def setup_inputs(seed: int = 0) -> dict:
    key_list = jax.random.split(jax.random.key(seed), 5)
    x_panel = draw_x_panel(jax.random.fold_in(key_list[4], 71), 0)
    grad_out = draw_grad_out(jax.random.fold_in(key_list[4], 71), 0)
    row_state = draw_row_state(jax.random.fold_in(key_list[4], 71), 0)
    col_state = draw_col_state(jax.random.fold_in(key_list[4], 71), 0)
    return dict(x_panel=x_panel, grad_out=grad_out, row_state=row_state, col_state=col_state)


def reference(x_panel, grad_out, row_state, col_state):
    gradient = jnp.stack([jnp.dot(x_panel.T, grad_out[0], preferred_element_type=jnp.float32), jnp.dot(x_panel.T, grad_out[1], preferred_element_type=jnp.float32)])
    squares = gradient * gradient + 1e-30
    new_rows = 0.7 * row_state + 0.3 * lax.optimization_barrier(jnp.mean(squares, axis=2))
    new_cols = 0.7 * col_state + 0.3 * lax.optimization_barrier(jnp.mean(squares, axis=1))
    row_level = lax.optimization_barrier(jnp.mean(new_rows, axis=1))
    update = gradient * lax.rsqrt(new_rows[:, :, None] * new_cols[:, None, :] / row_level[:, None, None])
    urms = jnp.sqrt(lax.optimization_barrier(jnp.mean(update * update, axis=(1, 2))))
    direction = update / jnp.maximum(1.0, urms)[:, None, None]
    return (direction, new_rows, new_cols)
```

```python
import jax
import jax.numpy as jnp
from jax import lax
from jax.experimental import pallas as pl
from jax.experimental.pallas import tpu as pltpu
from jax.sharding import PartitionSpec as P

D = 4096
FF = 10240
NZ = 16
NC = 32
TB = 512
XB = 256
FB = 256
HB = 320
W = 2 * HB
CH = 4
CT = TB // CH
START = 4

MESH = pl.DeviceIdType.MESH
f32 = jnp.float32


def kernel(
    x_hbm, g_hbm, rs_ref, cs_ref,
    grad_hbm, nr_ref, nc_ref, k_ref,
    gin, gbuf, xbuf, acc, split, rowx, colx, ux, s3x,
    lsem, grecv, gright, gleft, xrecv, xsend,
    rrecv, rsend, crecv, csend, urecv, usend, srecv, ssend,
):
    z = lax.axis_index("row")
    c = lax.axis_index("col")
    right = lax.rem(z + 1, NZ)
    left = lax.rem(z + NZ - 1, NZ)

    gcopy = [
        pltpu.make_async_copy(g_hbm.at[m], gin.at[m], lsem.at[m]) for m in range(2)
    ]
    xcopy = pltpu.make_async_copy(x_hbm, xbuf.at[c], lsem.at[2])
    for cp in gcopy:
        cp.start()
    xcopy.start()

    barrier = pltpu.get_barrier_semaphore()

    @pl.loop(1, NZ)
    def _(k):
        pl.semaphore_signal(
            barrier, inc=1, device_id=(lax.rem(z + k, NZ), c), device_id_type=MESH
        )

    @pl.loop(1, NC)
    def _(k):
        pl.semaphore_signal(
            barrier, inc=1, device_id=(z, lax.rem(c + k, NC)), device_id_type=MESH
        )

    pl.semaphore_wait(barrier, NZ - 1 + NC - 1)

    def piece(b, p):
        return gbuf.at[b, pl.ds(p * CT, CT), :]

    def hop(b, p, to_right):
        sems = gright if to_right else gleft
        return pltpu.make_async_remote_copy(
            src_ref=piece(b, p),
            dst_ref=piece(b, p),
            send_sem=sems.at[b, p],
            recv_sem=grecv.at[b, p],
            device_id=(right if to_right else left, c),
            device_id_type=MESH,
        )

    for cp in gcopy:
        cp.wait()
    for p in range(CH):
        rows = pl.ds(p * CT, CT)
        gbuf[z, rows, :] = jnp.concatenate([gin[0, rows, :], gin[1, rows, :]], axis=1)
        hop(z, p, True).start()
        hop(z, p, False).start()

    xcopy.wait()

    def xput(k):
        t = lax.rem(c + k, NC)
        return pltpu.make_async_remote_copy(
            src_ref=xbuf.at[c], dst_ref=xbuf.at[c],
            send_sem=xsend.at[k], recv_sem=xrecv.at[k],
            device_id=(z, t), device_id_type=MESH,
        )

    def xget(k):
        o = lax.rem(c + NC - k, NC)
        return pltpu.make_async_remote_copy(
            src_ref=xbuf.at[o], dst_ref=xbuf.at[o],
            send_sem=xsend.at[k], recv_sem=xrecv.at[k],
            device_id=(z, o), device_id_type=MESH,
        )

    @pl.loop(1, NC)
    def _(k):
        xput(k).start()

    acc[...] = jnp.zeros_like(acc)

    def mm(b):
        xa = jnp.concatenate([xbuf[2 * b], xbuf[2 * b + 1]], axis=0)
        acc[...] += lax.dot_general(
            xa, gbuf[b], (((0,), (0,)), ((), ())), preferred_element_type=f32
        )

    def mm_piece(b, p):
        per = XB // CT
        xa = xbuf[2 * b + p // per, pl.ds((p % per) * CT, CT), :]
        acc[...] += lax.dot_general(
            xa, gbuf[b, pl.ds(p * CT, CT), :], (((0,), (0,)), ((), ())),
            preferred_element_type=f32,
        )

    def from_left(s):
        return lax.rem(z + NZ - s, NZ)

    def from_right(s):
        return lax.rem(z + s, NZ)

    @pl.loop(1, START)
    def _(s):
        bl, br = from_left(s), from_right(s)
        for p in range(CH):
            hop(bl, p, True).wait_recv()
            hop(bl, p, True).start()
            hop(br, p, False).wait_recv()
            hop(br, p, False).start()

    @pl.loop(1, NC)
    def _(k):
        xget(k).wait_recv()

    @pl.loop(START, 7)
    def _(s):
        bl, br = from_left(s), from_right(s)
        q = 2 * (s - START)
        for p in range(CH):
            hop(bl, p, True).wait_recv()
            hop(bl, p, True).start()
            hop(br, p, False).wait_recv()
            hop(br, p, False).start()
            if p == 0:
                mm(from_left(q))
            elif p == 1:
                @pl.when(q > 0)
                def _():
                    mm(from_right(q))
            elif p == 2:
                mm(from_left(q + 1))
            elif p == 3:
                mm(from_right(q + 1))

    bl, br = from_left(7), from_right(7)
    for p in range(CH):
        hop(bl, p, True).wait_recv()
        if p < CH // 2:
            hop(bl, p, True).start()
        hop(br, p, False).wait_recv()
        if p >= CH // 2:
            hop(br, p, False).start()
        if p == 0:
            mm(from_left(6))
        elif p == 1:
            mm(from_right(6))
    mm(bl)
    mm(br)

    far = from_right(8)
    for p in range(CH // 2):
        for pp, to_right in ((p, True), (p + CH // 2, False)):
            hop(far, pp, to_right).wait_recv()
            mm_piece(far, pp)

    rsum = []
    for m in range(2):
        gm = acc[:, m * HB : (m + 1) * HB]
        split[m] = gm
        rsum.append(jnp.sum(gm * gm + 1e-30, axis=1, keepdims=True))
    lane = lax.broadcasted_iota(jnp.int32, (FB, 128), 1)
    rmat = jnp.where(lane == 0, rsum[0], rsum[1])
    rmat_t = rmat.T
    rowx[c, :, 0:FB] = rmat_t[0:1]
    rowx[c, :, FB : 2 * FB] = rmat_t[1:2]

    def put(buf, sends, recvs, k, along_row):
        if along_row:
            me, dev = z, (lax.rem(z + k, NZ), c)
        else:
            me, dev = c, (z, lax.rem(c + k, NC))
        return pltpu.make_async_remote_copy(
            src_ref=buf.at[me], dst_ref=buf.at[me],
            send_sem=sends.at[k], recv_sem=recvs.at[k],
            device_id=dev, device_id_type=MESH,
        )

    def get(buf, sends, recvs, k, along_row):
        if along_row:
            o = lax.rem(z + NZ - k, NZ)
            dev = (o, c)
        else:
            o = lax.rem(c + NC - k, NC)
            dev = (z, o)
        return pltpu.make_async_remote_copy(
            src_ref=buf.at[o], dst_ref=buf.at[o],
            send_sem=sends.at[k], recv_sem=recvs.at[k],
            device_id=dev, device_id_type=MESH,
        )

    def send_all(buf, sends, recvs, along_row):
        @pl.loop(1, NZ if along_row else NC)
        def _(k):
            put(buf, sends, recvs, k, along_row).start()

    def recv_all(buf, sends, recvs, along_row):
        @pl.loop(1, NZ if along_row else NC)
        def _(k):
            get(buf, sends, recvs, k, along_row).wait_recv()

    def drain(buf, sends, recvs, along_row):
        @pl.loop(1, NZ if along_row else NC)
        def _(k):
            put(buf, sends, recvs, k, along_row).wait_send()

    send_all(rowx, rsend, rrecv, False)

    out_copy = pltpu.make_async_copy(split, grad_hbm, lsem.at[3])
    out_copy.start()

    for m in range(2):
        gm = split[m]
        colx[z, :, m * 384 : m * 384 + HB] = jnp.sum(
            gm * gm + 1e-30, axis=0, keepdims=True
        )
    send_all(colx, csend, crecv, True)

    recv_all(rowx, rsend, rrecv, False)
    row_tot = jnp.sum(rowx[...], axis=0)
    nr = []
    for m in range(2):
        v = 0.7 * rs_ref[m : m + 1, :] + 0.3 * (row_tot[:, m * FB : (m + 1) * FB] / FF)
        nr_ref[m : m + 1, :] = v
        nr.append(v)
    sub = lax.broadcasted_iota(jnp.int32, (128, FB), 0)
    rcol = lax.rsqrt(jnp.where(sub == 0, nr[0], nr[1])).T
    lane1 = lax.broadcasted_iota(jnp.int32, (1, 128), 1)
    for m in range(2):
        u = split[m] * rcol[:, m : m + 1]
        ux[z, :, m * 384 : m * 384 + HB] = jnp.sum(u * u, axis=0, keepdims=True)
    level_part = jnp.where(
        lane1 == 0,
        jnp.sum(nr[0], axis=1, keepdims=True),
        jnp.sum(nr[1], axis=1, keepdims=True),
    )
    ux[z, :, 768:896] = level_part
    send_all(ux, usend, urecv, True)

    recv_all(colx, csend, crecv, True)
    col_tot = jnp.sum(colx[...], axis=0)
    nc = []
    for m in range(2):
        v = 0.7 * cs_ref[m : m + 1, :] + 0.3 * (col_tot[:, m * 384 : m * 384 + HB] / D)
        nc_ref[m : m + 1, :] = v
        nc.append(v)

    recv_all(ux, usend, urecv, True)
    u_tot = jnp.sum(ux[...], axis=0)
    s_part = [
        jnp.sum(u_tot[:, m * 384 : m * 384 + HB] / nc[m], axis=1, keepdims=True)
        for m in range(2)
    ]
    level = u_tot[:, 768:896] / D
    s3x[c] = jnp.where(lane1 == 0, s_part[0], s_part[1])
    send_all(s3x, ssend, srecv, False)
    recv_all(s3x, ssend, srecv, False)
    s_tot = jnp.sum(s3x[...], axis=0)
    urms = jnp.sqrt(level * (s_tot / (D * FF)))
    k_ref[...] = jnp.sqrt(level) / jnp.maximum(1.0, urms)

    drain(rowx, rsend, rrecv, False)
    drain(colx, csend, crecv, True)
    drain(ux, usend, urecv, True)
    drain(s3x, ssend, srecv, False)

    @pl.loop(1, NC)
    def _(k):
        xput(k).wait_send()

    @pl.loop(0, 7)
    def _(s):
        bl, br = from_left(s), from_right(s)
        for p in range(CH):
            hop(bl, p, True).wait_send()
            hop(br, p, False).wait_send()

    for p in range(CH // 2):
        hop(bl, p, True).wait_send()
        hop(br, p + CH // 2, False).wait_send()
    out_copy.wait()


def shards(x_panel, grad_out, row_state, col_state):
    vmem = pl.BlockSpec(memory_space=pltpu.VMEM)
    anym = pl.BlockSpec(memory_space=pl.ANY)
    dma = pltpu.SemaphoreType.DMA
    grad, new_rows, new_cols, k = pl.pallas_call(
        kernel,
        out_shape=(
            jax.ShapeDtypeStruct((2, FB, HB), f32),
            jax.ShapeDtypeStruct((2, FB), f32),
            jax.ShapeDtypeStruct((2, HB), f32),
            jax.ShapeDtypeStruct((1, 128), f32),
        ),
        in_specs=[anym, anym, vmem, vmem],
        out_specs=(anym, vmem, vmem, vmem),
        scratch_shapes=[
            pltpu.VMEM((2, TB, HB), jnp.bfloat16),
            pltpu.VMEM((NZ, TB, W), jnp.bfloat16),
            pltpu.VMEM((NC, XB, FB), jnp.bfloat16),
            pltpu.VMEM((FB, W), f32),
            pltpu.VMEM((2, FB, HB), f32),
            pltpu.VMEM((NC, 1, 2 * FB), f32),
            pltpu.VMEM((NZ, 1, 768), f32),
            pltpu.VMEM((NZ, 1, 896), f32),
            pltpu.VMEM((NC, 1, 128), f32),
            dma((4,)),
            dma((NZ, CH)),
            dma((NZ, CH)),
            dma((NZ, CH)),
            dma((NC,)),
            dma((NC,)),
            dma((NC,)),
            dma((NC,)),
            dma((NZ,)),
            dma((NZ,)),
            dma((NZ,)),
            dma((NZ,)),
            dma((NC,)),
            dma((NC,)),
        ],
        compiler_params=pltpu.CompilerParams(
            collective_id=0, has_side_effects=True, vmem_limit_bytes=56 * 1024 * 1024
        ),
        cost_estimate=pl.CostEstimate(
            flops=2 * D // NZ * W * 8192, bytes_accessed=3_000_000, transcendentals=0
        ),
    )(x_panel, grad_out, row_state, col_state)
    scale = k[0, :2]
    direction = (
        grad
        * (lax.rsqrt(new_rows) * scale[:, None])[:, :, None]
        * lax.rsqrt(new_cols)[:, None, :]
    )
    return (direction, new_rows, new_cols)


def solution(mesh):
    return jax.shard_map(
        shards,
        mesh=mesh,
        in_specs=(P("col", "row"), P(None, "row", "col"), P(None, "row"), P(None, "col")),
        out_specs=(P(None, "row", "col"), P(None, "row"), P(None, "col")),
        check_vma=False,
    )
```

```python
import jax
import jax.numpy as jnp
from jax import lax
from jax.experimental import pallas as pl
from jax.experimental.pallas import tpu as pltpu
from jax.sharding import PartitionSpec as P

D = 4096
FF = 10240
NZ = 16
NC = 32
NY = 4
NX = 4
TB = 512
XB = 256
FB = 256
HB = 320
W = 2 * HB
CH = 4
RP = W // CH
TAIL = True

MESH = pl.DeviceIdType.MESH
f32 = jnp.float32

Z_ORDER = sorted(range(1, NZ), key=lambda k: -min(k, NZ - k))
C_ORDER = sorted(
    range(1, NC),
    key=lambda k: -(min(k // 8, 4 - k // 8) + min(k // 2 % 4, 4 - k // 2 % 4)),
)


def kernel(
    x_hbm, g_hbm, rs_ref, cs_ref,
    upd_hbm, nr_ref, nc_ref, k_ref,
    gbuf, xbuf, acc, csv, rowx, colx, ux, s3x,
    lsem, grecv, gright, gleft, xsend, xrecv, esend, erecv,
):
    z = lax.axis_index("row")
    c = lax.axis_index("col")
    core = lax.rem(c, 2)
    chip = c // 2
    x = lax.rem(chip, NX)
    y = chip // NX
    right = lax.rem(z + 1, NZ)
    left = lax.rem(z + NZ - 1, NZ)

    def at(yy, xx, cc):
        return (z, (yy * NX + xx) * 2 + cc)

    xp, xm = lax.rem(x + 1, NX), lax.rem(x + NX - 1, NX)
    yp, ym = lax.rem(y + 1, NY), lax.rem(y + NY - 1, NY)
    half = pl.ds(core * XB, XB)

    gcopy = pltpu.make_async_copy(g_hbm, gbuf.at[z], lsem.at[0])
    xcopy = pltpu.make_async_copy(x_hbm, xbuf.at[chip, half, :], lsem.at[1])
    gcopy.start()
    xcopy.start()

    near = [
        (right, c), (left, c),
        at(y, xp, core), at(y, xm, core), at(yp, x, core), at(ym, x, core),
        at(y, x, 1 - core),
    ]
    barrier = pltpu.get_barrier_semaphore()
    for dev in near:
        pl.semaphore_signal(barrier, inc=1, device_id=dev, device_id_type=MESH)
    pl.semaphore_wait(barrier, len(near))

    def hop(b, p, to_right):
        sems = gright if to_right else gleft
        part = gbuf.at[b, pl.ds(p * RP, RP), :]
        return pltpu.make_async_remote_copy(
            src_ref=part,
            dst_ref=part,
            send_sem=sems.at[b, p],
            recv_sem=grecv.at[b, p],
            device_id=(right if to_right else left, c),
            device_id_type=MESH,
        )

    gcopy.wait()
    for p in range(CH):
        hop(z, p, True).start()
        hop(z, p, False).start()

    def xmove(i, first, count, half, dev):
        ref = xbuf.at[pl.ds(first, count), half, :]
        return pltpu.make_async_remote_copy(
            src_ref=ref, dst_ref=ref, send_sem=xsend.at[i], recv_sem=xrecv.at[i],
            device_id=dev, device_id_type=MESH,
        )

    xx2 = lax.rem(x + 2, NX)
    yy2 = lax.rem(y + 2, NY)
    to_xp, to_xm = at(y, xp, core), at(y, xm, core)
    to_yp, to_ym = at(yp, x, core), at(ym, x, core)
    row0 = y * NX
    outgoing = [
        xmove(0, chip, 1, half, to_xp),
        xmove(1, chip, 1, half, to_xm),
        xmove(2, row0 + xm, 1, half, to_xp),
        xmove(3, row0, NX, half, to_yp),
        xmove(4, row0, NX, half, to_ym),
        xmove(5, ym * NX, NX // 2, half, to_yp),
        xmove(6, yp * NX + NX // 2, NX // 2, half, to_ym),
        xmove(7, 0, NX * NY, half, at(y, x, 1 - core)),
    ]
    other = pl.ds((1 - core) * XB, XB)
    incoming = [
        xmove(0, row0 + xm, 1, half, to_xp),
        xmove(1, row0 + xp, 1, half, to_xm),
        xmove(2, row0 + xx2, 1, half, to_xp),
        xmove(3, ym * NX, NX, half, to_yp),
        xmove(4, yp * NX, NX, half, to_ym),
        xmove(5, yy2 * NX, NX // 2, half, to_yp),
        xmove(6, yy2 * NX + NX // 2, NX // 2, half, to_ym),
        xmove(7, 0, NX * NY, other, at(y, x, 1 - core)),
    ]
    x_rounds = [((0, 1), (2,)), ((2,), (3, 4)), ((3, 4), (5, 6)), ((5, 6), (7,)), ((7,), ())]

    xcopy.wait()
    outgoing[0].start()
    outgoing[1].start()

    acc[...] = jnp.zeros_like(acc)
    csv[:, :HB] = cs_ref[0:1, :]
    csv[:, HB:] = cs_ref[1:2, :]

    def mm(b):
        acc[...] += jnp.dot(gbuf[b], xbuf[b], preferred_element_type=f32)

    def mm_piece(b, p):
        rows = pl.ds(p * RP, RP)
        acc[rows, :] += jnp.dot(gbuf[b, rows, :], xbuf[b], preferred_element_type=f32)

    def from_left(s):
        return lax.rem(z + NZ - s, NZ)

    def from_right(s):
        return lax.rem(z + s, NZ)

    @pl.loop(1, 7)
    def _(s):
        bl, br = from_left(s), from_right(s)
        for p in range(CH):
            hop(bl, p, True).wait_recv()
            hop(bl, p, True).start()
            hop(br, p, False).wait_recv()
            hop(br, p, False).start()
        for i, (arrived, leaving) in enumerate(x_rounds):
            @pl.when(s == i + 1)
            def _():
                for j in arrived:
                    incoming[j].wait_recv()
                for j in leaving:
                    outgoing[j].start()

    mm(z)

    @pl.loop(1, 4)
    def _(q):
        mm(from_left(q))
        mm(from_right(q))

    bl, br = from_left(7), from_right(7)
    for p in range(CH):
        hop(bl, p, True).wait_recv()
        if p < CH // 2:
            hop(bl, p, True).start()
        hop(br, p, False).wait_recv()
        if p >= CH // 2:
            hop(br, p, False).start()
        if p < CH - 1:
            mm(from_left(4 + p))
            mm(from_right(4 + p))
    mm(bl)
    mm(br)

    far = from_right(8)
    for p in range(CH // 2):
        for pp, to_right in ((p, True), (p + CH // 2, False)):
            hop(far, pp, to_right).wait_recv()
            mm_piece(far, pp)

    def partner(k, along_row):
        if along_row:
            return (lax.rem(z + k, NZ), c)
        dy, dx, dc = k // 8, k // 2 % 4, k % 2
        return at(
            lax.rem(y + dy, NY), lax.rem(x + dx, NX), 1 - core if dc else core
        )

    def send_all(i, buf, along_row):
        for k in Z_ORDER if along_row else C_ORDER:
            pltpu.make_async_remote_copy(
                src_ref=buf.at[0], dst_ref=buf.at[k],
                send_sem=esend.at[i], recv_sem=erecv.at[i],
                device_id=partner(k, along_row), device_id_type=MESH,
            ).start()

    def whole(i, buf, along_row):
        ref = buf.at[pl.ds(1, (NZ if along_row else NC) - 1)]
        return pltpu.make_async_remote_copy(
            src_ref=ref, dst_ref=ref,
            send_sem=esend.at[i], recv_sem=erecv.at[i],
            device_id=partner(1, along_row), device_id_type=MESH,
        )

    for m in range(2):
        gm = acc[m * HB : (m + 1) * HB, :]
        rowx[0, :, m * FB : (m + 1) * FB] = jnp.sum(
            gm * gm + 1e-30, axis=0, keepdims=True
        )
    send_all(0, rowx, False)

    def over_features(v):
        folded = v[:, :128] + v[:, 128:]
        return jnp.sum(folded.T, axis=0, keepdims=True)

    a = acc[...]
    colx[0] = over_features(a * a + 1e-30)
    send_all(1, colx, True)

    for j in range(8):
        outgoing[j].wait_send()

    @pl.loop(0, 7)
    def _(s):
        bl, br = from_left(s), from_right(s)
        for p in range(CH):
            hop(bl, p, True).wait_send()
            hop(br, p, False).wait_send()

    for p in range(CH // 2):
        hop(bl, p, True).wait_send()
        hop(br, p + CH // 2, False).wait_send()

    whole(0, rowx, False).wait_recv()
    row_tot = jnp.sum(rowx[...], axis=0)
    nr = []
    lane = lax.broadcasted_iota(jnp.int32, (1, 128), 1)
    for m in range(2):
        v = 0.7 * rs_ref[m : m + 1, :] + 0.3 * (row_tot[:, m * FB : (m + 1) * FB] / FF)
        nr_ref[m : m + 1, :] = v
        nr.append(v)
    hid = lax.broadcasted_iota(jnp.int32, (W, FB), 0)
    u = acc[...] * jnp.where(hid < HB, lax.rsqrt(nr[0]), lax.rsqrt(nr[1]))
    ux[0, :, 0:W] = over_features(u * u)
    ux[0, :, W : W + 128] = jnp.where(
        lane == 0,
        jnp.sum(nr[0], axis=1, keepdims=True),
        jnp.sum(nr[1], axis=1, keepdims=True),
    )
    send_all(2, ux, True)
    acc[...] = u

    whole(1, colx, True).wait_recv()
    col_tot = jnp.sum(colx[...], axis=0)
    ncv = 0.7 * csv[...] + 0.3 * (col_tot / D)
    nc_ref[0:1, :] = ncv[:, :HB]
    nc_ref[1:2, :] = ncv[:, HB:]
    ccol = jnp.broadcast_to(lax.rsqrt(ncv), (128, W)).T
    acc[:, :128] = acc[:, :128] * ccol
    acc[:, 128:] = acc[:, 128:] * ccol
    ucopy = pltpu.make_async_copy(acc, upd_hbm, lsem.at[2])
    ucopy.start()

    whole(2, ux, True).wait_recv()
    u_tot = jnp.sum(ux[...], axis=0)
    share = u_tot[:, 0:W] / ncv
    first = lax.broadcasted_iota(jnp.int32, (1, W), 1) < HB
    s3x[0] = jnp.where(
        lane == 0,
        jnp.sum(jnp.where(first, share, 0.0), axis=1, keepdims=True),
        jnp.sum(jnp.where(first, 0.0, share), axis=1, keepdims=True),
    )
    send_all(3, s3x, False)
    level = u_tot[:, W : W + 128] / D
    whole(0, rowx, False).wait_send()
    whole(1, colx, True).wait_send()
    whole(2, ux, True).wait_send()
    ucopy.wait()
    whole(3, s3x, False).wait_recv()
    s_tot = jnp.sum(s3x[...], axis=0)
    urms = jnp.sqrt(level * (s_tot / (D * FF)))
    k_ref[...] = jnp.sqrt(level) / jnp.maximum(1.0, urms)
    whole(3, s3x, False).wait_send()


def finish(upd_ref, nr_in, nc_in, k_ref, out_ref, nr_ref, nc_ref):
    m = pl.program_id(0)
    k = k_ref[...]
    out_ref[...] = upd_ref[...] * jnp.where(m == 0, k[:, 0:1], k[:, 1:2])

    @pl.when(m == 0)
    def _():
        nr_ref[...] = nr_in[...]
        nc_ref[...] = nc_in[...]


def shards(x_panel, grad_out, row_state, col_state):
    vmem = pl.BlockSpec(memory_space=pltpu.VMEM)
    anym = pl.BlockSpec(memory_space=pl.ANY)
    dma = pltpu.SemaphoreType.DMA
    grad_t = jnp.swapaxes(grad_out, 1, 2).reshape(W, TB)
    upd, new_rows, new_cols, k = pl.pallas_call(
        kernel,
        out_shape=(
            jax.ShapeDtypeStruct((W, FB), f32),
            jax.ShapeDtypeStruct((2, FB), f32),
            jax.ShapeDtypeStruct((2, HB), f32),
            jax.ShapeDtypeStruct((1, 128), f32),
        ),
        in_specs=[anym, anym, vmem, vmem],
        out_specs=(anym, vmem, vmem, vmem),
        scratch_shapes=[
            pltpu.VMEM((NZ, W, TB), jnp.bfloat16),
            pltpu.VMEM((NZ, TB, FB), jnp.bfloat16),
            pltpu.VMEM((W, FB), f32),
            pltpu.VMEM((1, W), f32),
            pltpu.VMEM((NC, 1, 2 * FB), f32),
            pltpu.VMEM((NZ, 1, W), f32),
            pltpu.VMEM((NZ, 1, W + 128), f32),
            pltpu.VMEM((NC, 1, 128), f32),
            dma((3,)),
            dma((NZ, CH)),
            dma((NZ, CH)),
            dma((NZ, CH)),
            dma((8,)),
            dma((8,)),
            dma((4,)),
            dma((4,)),
        ],
        compiler_params=pltpu.CompilerParams(
            collective_id=0, has_side_effects=True, vmem_limit_bytes=56 * 1024 * 1024
        ),
        cost_estimate=pl.CostEstimate(
            flops=2 * FB * W * 8192, bytes_accessed=3_000_000, transcendentals=0
        ),
    )(x_panel, grad_t, row_state, col_state)
    half = pl.BlockSpec((HB, FB), lambda m: (m, 0))
    direction, new_rows, new_cols = pl.pallas_call(
        finish,
        grid=(2,),
        out_shape=(
            jax.ShapeDtypeStruct((W, FB), f32),
            jax.ShapeDtypeStruct((2, FB), f32),
            jax.ShapeDtypeStruct((2, HB), f32),
        ),
        in_specs=[half, vmem, vmem, vmem],
        out_specs=(half, vmem, vmem),
    )(upd, new_rows, new_cols, k)
    direction = jnp.swapaxes(direction.reshape(2, HB, FB), 1, 2)
    return (direction, new_rows, new_cols)


def solution(mesh):
    return jax.shard_map(
        shards,
        mesh=mesh,
        in_specs=(P("col", "row"), P(None, "row", "col"), P(None, "row"), P(None, "col")),
        out_specs=(P(None, "row", "col"), P(None, "row"), P(None, "col")),
        check_vma=False,
    )
```

```python
import jax
import jax.numpy as jnp
from jax import lax
from jax.experimental import pallas as pl
from jax.experimental.pallas import tpu as pltpu
from jax.sharding import PartitionSpec as P

D = 4096
FF = 10240
NZ = 16
NC = 32
NY = 4
NX = 4
TB = 512
XB = 256
FB = 256
HB = 320
W = 2 * HB
CH = 2
RP = W // CH
QS = 4
QP = W // QS

MESH = pl.DeviceIdType.MESH
f32 = jnp.float32

Z_ORDER = sorted(range(1, NZ), key=lambda k: -min(k, NZ - k))
C_ORDER = sorted(
    range(1, NC),
    key=lambda k: -(min(k // 8, 4 - k // 8) + min(k // 2 % 4, 4 - k // 2 % 4)),
)


def kernel(
    x_hbm, g_hbm, rs_ref, cs_ref,
    upd_hbm, nr_ref, nc_ref, k_ref,
    gbuf, xbuf, acc, csv, rowx, colx, ux, s3x,
    lsem, grecv, gright, gleft, xsend, xrecv, esend, erecv,
):
    z = lax.axis_index("row")
    c = lax.axis_index("col")
    core = lax.rem(c, 2)
    chip = c // 2
    x = lax.rem(chip, NX)
    y = chip // NX
    right = lax.rem(z + 1, NZ)
    left = lax.rem(z + NZ - 1, NZ)

    def at(yy, xx, cc):
        return (z, (yy * NX + xx) * 2 + cc)

    xp, xm = lax.rem(x + 1, NX), lax.rem(x + NX - 1, NX)
    yp, ym = lax.rem(y + 1, NY), lax.rem(y + NY - 1, NY)
    half = pl.ds(core * XB, XB)

    gcopy = pltpu.make_async_copy(g_hbm, gbuf.at[z], lsem.at[0])
    xcopy = pltpu.make_async_copy(x_hbm, xbuf.at[chip, half, :], lsem.at[1])
    near = [
        (right, c), (left, c),
        at(y, xp, core), at(y, xm, core), at(yp, x, core), at(ym, x, core),
        at(y, x, 1 - core),
    ]
    barrier = pltpu.get_barrier_semaphore()
    for dev in near:
        pl.semaphore_signal(barrier, inc=1, device_id=dev, device_id_type=MESH)
    gcopy.start()
    xcopy.start()
    pl.semaphore_wait(barrier, len(near))

    def hop(b, p, to_right, own=False):
        sems = gright if to_right else gleft
        part = gbuf.at[b, pl.ds(p * RP, RP), :]
        return pltpu.make_async_remote_copy(
            src_ref=g_hbm.at[pl.ds(p * RP, RP), :] if own else part,
            dst_ref=part,
            send_sem=sems.at[b, p],
            recv_sem=grecv.at[b, p],
            device_id=(right if to_right else left, c),
            device_id_type=MESH,
        )

    for p in range(CH):
        hop(z, p, True, own=True).start()
        hop(z, p, False, own=True).start()

    def xmove(i, first, count, half, dev):
        ref = xbuf.at[pl.ds(first, count), half, :]
        return pltpu.make_async_remote_copy(
            src_ref=ref, dst_ref=ref, send_sem=xsend.at[i], recv_sem=xrecv.at[i],
            device_id=dev, device_id_type=MESH,
        )

    xx2 = lax.rem(x + 2, NX)
    yy2 = lax.rem(y + 2, NY)
    to_xp, to_xm = at(y, xp, core), at(y, xm, core)
    to_yp, to_ym = at(yp, x, core), at(ym, x, core)
    row0 = y * NX
    outgoing = [
        xmove(0, chip, 1, half, to_xp),
        xmove(1, chip, 1, half, to_xm),
        xmove(2, row0 + xm, 1, half, to_xp),
        xmove(3, row0, NX, half, to_yp),
        xmove(4, row0, NX, half, to_ym),
        xmove(5, ym * NX, NX // 2, half, to_yp),
        xmove(6, yp * NX + NX // 2, NX // 2, half, to_ym),
        xmove(7, 0, NX * NY, half, at(y, x, 1 - core)),
    ]
    other = pl.ds((1 - core) * XB, XB)
    incoming = [
        xmove(0, row0 + xm, 1, half, to_xp),
        xmove(1, row0 + xp, 1, half, to_xm),
        xmove(2, row0 + xx2, 1, half, to_xp),
        xmove(3, ym * NX, NX, half, to_yp),
        xmove(4, yp * NX, NX, half, to_ym),
        xmove(5, yy2 * NX, NX // 2, half, to_yp),
        xmove(6, yy2 * NX + NX // 2, NX // 2, half, to_ym),
        xmove(7, 0, NX * NY, other, at(y, x, 1 - core)),
    ]
    x_rounds = [((0, 1), (2,)), ((2,), (3, 4)), ((3, 4), (5, 6)), ((5, 6), (7,)), ((7,), ())]

    xcopy.wait()
    outgoing[0].start()
    outgoing[1].start()

    acc[...] = jnp.zeros_like(acc)
    csv[:, :HB] = cs_ref[0:1, :]
    csv[:, HB:] = cs_ref[1:2, :]

    def mm(b):
        acc[...] += jnp.dot(gbuf[b], xbuf[b], preferred_element_type=f32)

    def mm_piece(b, p):
        rows = pl.ds(p * RP, RP)
        acc[rows, :] += jnp.dot(gbuf[b, rows, :], xbuf[b], preferred_element_type=f32)

    def from_left(s):
        return lax.rem(z + NZ - s, NZ)

    def from_right(s):
        return lax.rem(z + s, NZ)

    @pl.loop(1, 7)
    def _(s):
        bl, br = from_left(s), from_right(s)
        for p in range(CH):
            hop(bl, p, True).wait_recv()
            hop(bl, p, True).start()
            hop(br, p, False).wait_recv()
            hop(br, p, False).start()
        for i, (arrived, leaving) in enumerate(x_rounds):
            @pl.when(s == i + 1)
            def _():
                for j in arrived:
                    incoming[j].wait_recv()
                for j in leaving:
                    outgoing[j].start()

    gcopy.wait()
    mm(z)

    @pl.loop(1, 4)
    def _(q):
        mm(from_left(q))
        mm(from_right(q))

    bl, br = from_left(7), from_right(7)
    for p in range(CH):
        hop(bl, p, True).wait_recv()
        if p < CH // 2:
            hop(bl, p, True).start()
        hop(br, p, False).wait_recv()
        if p >= CH // 2:
            hop(br, p, False).start()
        if p == 0:
            for q in (4, 5):
                mm(from_left(q))
                mm(from_right(q))
    for q in (6, 7):
        mm(from_left(q))
        mm(from_right(q))

    far = from_right(8)
    for m, to_right in ((0, True), (1, False)):
        hop(far, m, to_right).wait_recv()
        mm_piece(far, m)
        gm = acc[m * HB : (m + 1) * HB, :]
        rowx[0, :, m * FB : (m + 1) * FB] = jnp.sum(
            gm * gm + 1e-30, axis=0, keepdims=True
        )

    def partner(k, along_row):
        if along_row:
            return (lax.rem(z + k, NZ), c)
        dy, dx, dc = k // 8, k // 2 % 4, k % 2
        return at(
            lax.rem(y + dy, NY), lax.rem(x + dx, NX), 1 - core if dc else core
        )

    def send_all(i, buf, along_row):
        for k in Z_ORDER if along_row else C_ORDER:
            pltpu.make_async_remote_copy(
                src_ref=buf.at[0], dst_ref=buf.at[k],
                send_sem=esend.at[i], recv_sem=erecv.at[i],
                device_id=partner(k, along_row), device_id_type=MESH,
            ).start()

    def whole(i, buf, along_row):
        ref = buf.at[pl.ds(1, (NZ if along_row else NC) - 1)]
        return pltpu.make_async_remote_copy(
            src_ref=ref, dst_ref=ref,
            send_sem=esend.at[i], recv_sem=erecv.at[i],
            device_id=partner(1, along_row), device_id_type=MESH,
        )

    send_all(0, rowx, False)

    def over_features(v):
        folded = v[:, :128] + v[:, 128:]
        return jnp.sum(folded.T, axis=0, keepdims=True)

    a = acc[...]
    colx[0] = over_features(a * a + 1e-30)
    send_all(1, colx, True)

    for j in range(8):
        outgoing[j].wait_send()

    for p in range(CH):
        hop(z, p, True, own=True).wait_send()
        hop(z, p, False, own=True).wait_send()

    @pl.loop(1, 7)
    def _(s):
        bl, br = from_left(s), from_right(s)
        for p in range(CH):
            hop(bl, p, True).wait_send()
            hop(br, p, False).wait_send()

    for p in range(CH // 2):
        hop(bl, p, True).wait_send()
        hop(br, p + CH // 2, False).wait_send()

    whole(0, rowx, False).wait_recv()
    row_tot = jnp.sum(rowx[...], axis=0)
    nr = []
    lane = lax.broadcasted_iota(jnp.int32, (1, 128), 1)
    for m in range(2):
        v = 0.7 * rs_ref[m : m + 1, :] + 0.3 * (row_tot[:, m * FB : (m + 1) * FB] / FF)
        nr_ref[m : m + 1, :] = v
        nr.append(v)
    hid = lax.broadcasted_iota(jnp.int32, (W, FB), 0)
    u = acc[...] * jnp.where(hid < HB, lax.rsqrt(nr[0]), lax.rsqrt(nr[1]))
    ux[0, :, 0:W] = over_features(u * u)
    ux[0, :, W : W + 128] = jnp.where(
        lane == 0,
        jnp.sum(nr[0], axis=1, keepdims=True),
        jnp.sum(nr[1], axis=1, keepdims=True),
    )
    send_all(2, ux, True)
    acc[...] = u

    whole(1, colx, True).wait_recv()
    col_tot = jnp.sum(colx[...], axis=0)
    ncv = 0.7 * csv[...] + 0.3 * (col_tot / D)
    nc_ref[0:1, :] = ncv[:, :HB]
    nc_ref[1:2, :] = ncv[:, HB:]
    ccol = jnp.broadcast_to(lax.rsqrt(ncv), (128, W)).T
    acc[:, :128] = acc[:, :128] * ccol
    acc[:, 128:] = acc[:, 128:] * ccol
    ucopy = pltpu.make_async_copy(acc, upd_hbm, lsem.at[2])
    ucopy.start()

    whole(2, ux, True).wait_recv()
    u_tot = jnp.sum(ux[...], axis=0)
    share = u_tot[:, 0:W] / ncv
    first = lax.broadcasted_iota(jnp.int32, (1, W), 1) < HB
    s3x[0] = jnp.where(
        lane == 0,
        jnp.sum(jnp.where(first, share, 0.0), axis=1, keepdims=True),
        jnp.sum(jnp.where(first, 0.0, share), axis=1, keepdims=True),
    )
    send_all(3, s3x, False)
    level = u_tot[:, W : W + 128] / D
    whole(0, rowx, False).wait_send()
    whole(1, colx, True).wait_send()
    whole(2, ux, True).wait_send()
    ucopy.wait()
    whole(3, s3x, False).wait_recv()
    s_tot = jnp.sum(s3x[...], axis=0)
    urms = jnp.sqrt(level * (s_tot / (D * FF)))
    k_ref[...] = jnp.sqrt(level) / jnp.maximum(1.0, urms)
    whole(3, s3x, False).wait_send()


def finish(
    upd_hbm, nr_hbm, nc_hbm, k_hbm, out_hbm, nr_out, nc_out,
    buf, nr, nc, k, in_sem, out_sem,
):
    def piece(ref, i):
        return ref.at[pl.ds(i * QP, QP), :]

    copy = pltpu.make_async_copy
    ins = [copy(k_hbm, k, in_sem.at[QS])]
    ins += [copy(piece(upd_hbm, i), piece(buf, i), in_sem.at[i]) for i in range(QS)]
    small = [copy(nr_hbm, nr, in_sem.at[QS + 1]), copy(nc_hbm, nc, in_sem.at[QS + 2])]
    for cp in ins + small:
        cp.start()
    outs = [copy(piece(buf, i), piece(out_hbm, i), out_sem.at[i]) for i in range(QS)]
    outs += [copy(nr, nr_out, out_sem.at[QS]), copy(nc, nc_out, out_sem.at[QS + 1])]
    ins[0].wait()
    scale = k[...]
    for i in range(QS):
        ins[1 + i].wait()
        m = i // (QS // 2)
        rows = pl.ds(i * QP, QP)
        buf[rows, :] = buf[rows, :] * scale[:, m : m + 1]
        outs[i].start()
    for cp, out in zip(small, outs[QS:]):
        cp.wait()
        out.start()
    for out in outs:
        out.wait()


def shards(x_panel, grad_out, row_state, col_state):
    vmem = pl.BlockSpec(memory_space=pltpu.VMEM)
    anym = pl.BlockSpec(memory_space=pl.ANY)
    dma = pltpu.SemaphoreType.DMA
    grad_t = jnp.swapaxes(grad_out, 1, 2).reshape(W, TB)
    upd, new_rows, new_cols, k = pl.pallas_call(
        kernel,
        out_shape=(
            jax.ShapeDtypeStruct((W, FB), f32),
            jax.ShapeDtypeStruct((2, FB), f32),
            jax.ShapeDtypeStruct((2, HB), f32),
            jax.ShapeDtypeStruct((1, 128), f32),
        ),
        in_specs=[anym, anym, vmem, vmem],
        out_specs=(anym, vmem, vmem, vmem),
        scratch_shapes=[
            pltpu.VMEM((NZ, W, TB), jnp.bfloat16),
            pltpu.VMEM((NZ, TB, FB), jnp.bfloat16),
            pltpu.VMEM((W, FB), f32),
            pltpu.VMEM((1, W), f32),
            pltpu.VMEM((NC, 1, 2 * FB), f32),
            pltpu.VMEM((NZ, 1, W), f32),
            pltpu.VMEM((NZ, 1, W + 128), f32),
            pltpu.VMEM((NC, 1, 128), f32),
            dma((3,)),
            dma((NZ, CH)),
            dma((NZ, CH)),
            dma((NZ, CH)),
            dma((8,)),
            dma((8,)),
            dma((4,)),
            dma((4,)),
        ],
        compiler_params=pltpu.CompilerParams(
            collective_id=0, has_side_effects=True, vmem_limit_bytes=56 * 1024 * 1024
        ),
        cost_estimate=pl.CostEstimate(
            flops=2 * FB * W * 8192, bytes_accessed=3_000_000, transcendentals=0
        ),
    )(x_panel, grad_t, row_state, col_state)
    direction, new_rows, new_cols = pl.pallas_call(
        finish,
        out_shape=(
            jax.ShapeDtypeStruct((W, FB), f32),
            jax.ShapeDtypeStruct((2, FB), f32),
            jax.ShapeDtypeStruct((2, HB), f32),
        ),
        in_specs=[anym, anym, anym, anym],
        out_specs=(anym, anym, anym),
        scratch_shapes=[
            pltpu.VMEM((W, FB), f32),
            pltpu.VMEM((2, FB), f32),
            pltpu.VMEM((2, HB), f32),
            pltpu.VMEM((1, 128), f32),
            dma((QS + 3,)),
            dma((QS + 2,)),
        ],
    )(upd, new_rows, new_cols, k)
    direction = jnp.swapaxes(direction.reshape(2, HB, FB), 1, 2)
    return (direction, new_rows, new_cols)


def solution(mesh):
    return jax.shard_map(
        shards,
        mesh=mesh,
        in_specs=(P("col", "row"), P(None, "row", "col"), P(None, "row"), P(None, "col")),
        out_specs=(P(None, "row", "col"), P(None, "row"), P(None, "col")),
        check_vma=False,
    )
```

```python
import jax
import jax.numpy as jnp
from jax import lax
from jax.experimental import pallas as pl
from jax.experimental.pallas import tpu as pltpu
from jax.sharding import PartitionSpec as P

D = 4096
FF = 10240
NZ = 16
NC = 32
NY = 4
NX = 4
TB = 512
XB = 256
FB = 256
HB = 320
W = 2 * HB
CH = 2
RP = W // CH
QS = 4
QP = W // QS

MESH = pl.DeviceIdType.MESH
f32 = jnp.float32

Z_ORDER = sorted(range(1, NZ), key=lambda k: -min(k, NZ - k))
C_ORDER = sorted(
    range(1, NC),
    key=lambda k: -(min(k // 8, 4 - k // 8) + min(k // 2 % 4, 4 - k // 2 % 4)),
)


def kernel(
    x_hbm, g_hbm, rs_ref, cs_ref,
    upd_hbm, nr_ref, nc_ref, k_ref,
    gbuf, xbuf, acc, csv, rowx, colx, ux, s3x,
    lsem, grecv, gright, gleft, xsend, xrecv, esend, erecv,
):
    z = lax.axis_index("row")
    c = lax.axis_index("col")
    core = lax.rem(c, 2)
    chip = c // 2
    x = lax.rem(chip, NX)
    y = chip // NX
    right = lax.rem(z + 1, NZ)
    left = lax.rem(z + NZ - 1, NZ)

    def at(yy, xx, cc):
        return (z, (yy * NX + xx) * 2 + cc)

    xp, xm = lax.rem(x + 1, NX), lax.rem(x + NX - 1, NX)
    yp, ym = lax.rem(y + 1, NY), lax.rem(y + NY - 1, NY)
    half = pl.ds(core * XB, XB)

    gcopy = pltpu.make_async_copy(g_hbm, gbuf.at[z], lsem.at[0])
    xcopy = pltpu.make_async_copy(x_hbm, xbuf.at[chip, half, :], lsem.at[1])
    near = [
        (right, c), (left, c),
        at(y, xp, core), at(y, xm, core), at(yp, x, core), at(ym, x, core),
        at(y, x, 1 - core),
    ]
    barrier = pltpu.get_barrier_semaphore()
    for dev in near:
        pl.semaphore_signal(barrier, inc=1, device_id=dev, device_id_type=MESH)
    gcopy.start()
    xcopy.start()
    pl.semaphore_wait(barrier, len(near))

    def hop(b, p, to_right, own=False):
        sems = gright if to_right else gleft
        part = gbuf.at[b, pl.ds(p * RP, RP), :]
        return pltpu.make_async_remote_copy(
            src_ref=g_hbm.at[pl.ds(p * RP, RP), :] if own else part,
            dst_ref=part,
            send_sem=sems.at[b, p],
            recv_sem=grecv.at[b, p],
            device_id=(right if to_right else left, c),
            device_id_type=MESH,
        )

    for p in range(CH):
        hop(z, p, True, own=True).start()
        hop(z, CH - 1 - p, False, own=True).start()

    def xmove(i, first, count, half, dev):
        ref = xbuf.at[pl.ds(first, count), half, :]
        return pltpu.make_async_remote_copy(
            src_ref=ref, dst_ref=ref, send_sem=xsend.at[i], recv_sem=xrecv.at[i],
            device_id=dev, device_id_type=MESH,
        )

    xx2 = lax.rem(x + 2, NX)
    yy2 = lax.rem(y + 2, NY)
    to_xp, to_xm = at(y, xp, core), at(y, xm, core)
    to_yp, to_ym = at(yp, x, core), at(ym, x, core)
    row0 = y * NX
    outgoing = [
        xmove(0, chip, 1, half, to_xp),
        xmove(1, chip, 1, half, to_xm),
        xmove(2, row0 + xm, 1, half, to_xp),
        xmove(3, row0, NX, half, to_yp),
        xmove(4, row0, NX, half, to_ym),
        xmove(5, ym * NX, NX // 2, half, to_yp),
        xmove(6, yp * NX + NX // 2, NX // 2, half, to_ym),
        xmove(7, 0, NX * NY, half, at(y, x, 1 - core)),
    ]
    other = pl.ds((1 - core) * XB, XB)
    incoming = [
        xmove(0, row0 + xm, 1, half, to_xp),
        xmove(1, row0 + xp, 1, half, to_xm),
        xmove(2, row0 + xx2, 1, half, to_xp),
        xmove(3, ym * NX, NX, half, to_yp),
        xmove(4, yp * NX, NX, half, to_ym),
        xmove(5, yy2 * NX, NX // 2, half, to_yp),
        xmove(6, yy2 * NX + NX // 2, NX // 2, half, to_ym),
        xmove(7, 0, NX * NY, other, at(y, x, 1 - core)),
    ]
    x_rounds = [((0, 1), (2,)), ((2,), (3, 4)), ((3, 4), (5, 6)), ((5, 6), (7,)), ((7,), ())]

    xcopy.wait()
    outgoing[0].start()
    outgoing[1].start()

    acc[...] = jnp.zeros_like(acc)
    csv[:, :HB] = cs_ref[0:1, :]
    csv[:, HB:] = cs_ref[1:2, :]

    def mm(b):
        acc[...] += jnp.dot(gbuf[b], xbuf[b], preferred_element_type=f32)

    def mm_piece(b, p):
        rows = pl.ds(p * RP, RP)
        acc[rows, :] += jnp.dot(gbuf[b, rows, :], xbuf[b], preferred_element_type=f32)

    def from_left(s):
        return lax.rem(z + NZ - s, NZ)

    def from_right(s):
        return lax.rem(z + s, NZ)

    @pl.loop(1, 7)
    def _(s):
        bl, br = from_left(s), from_right(s)
        for p in range(CH):
            hop(bl, p, True).wait_recv()
            hop(bl, p, True).start()
            hop(br, CH - 1 - p, False).wait_recv()
            hop(br, CH - 1 - p, False).start()
        for i, (arrived, leaving) in enumerate(x_rounds):
            @pl.when(s == i + 1)
            def _():
                for j in arrived:
                    incoming[j].wait_recv()
                for j in leaving:
                    outgoing[j].start()

    gcopy.wait()
    mm(z)

    @pl.loop(1, 4)
    def _(q):
        mm(from_left(q))
        mm(from_right(q))

    bl, br = from_left(7), from_right(7)
    for p in range(CH):
        hop(bl, p, True).wait_recv()
        if p < CH // 2:
            hop(bl, p, True).start()
        hop(br, CH - 1 - p, False).wait_recv()
        if p < CH // 2:
            hop(br, CH - 1 - p, False).start()
        if p == 0:
            for q in (4, 5):
                mm(from_left(q))
                mm(from_right(q))
    for q in (6, 7):
        mm(from_left(q))
        mm(from_right(q))

    far = from_right(8)
    for m, to_right in ((0, True), (1, False)):
        hop(far, m, to_right).wait_recv()
        mm_piece(far, m)
        gm = acc[m * HB : (m + 1) * HB, :]
        rowx[0, :, m * FB : (m + 1) * FB] = jnp.sum(
            gm * gm + 1e-30, axis=0, keepdims=True
        )

    def partner(k, along_row):
        if along_row:
            return (lax.rem(z + k, NZ), c)
        dy, dx, dc = k // 8, k // 2 % 4, k % 2
        return at(
            lax.rem(y + dy, NY), lax.rem(x + dx, NX), 1 - core if dc else core
        )

    def send_all(i, buf, along_row):
        for k in Z_ORDER if along_row else C_ORDER:
            pltpu.make_async_remote_copy(
                src_ref=buf.at[0], dst_ref=buf.at[k],
                send_sem=esend.at[i], recv_sem=erecv.at[i],
                device_id=partner(k, along_row), device_id_type=MESH,
            ).start()

    def whole(i, buf, along_row):
        ref = buf.at[pl.ds(1, (NZ if along_row else NC) - 1)]
        return pltpu.make_async_remote_copy(
            src_ref=ref, dst_ref=ref,
            send_sem=esend.at[i], recv_sem=erecv.at[i],
            device_id=partner(1, along_row), device_id_type=MESH,
        )

    send_all(0, rowx, False)

    def over_features(v):
        folded = v[:, :128] + v[:, 128:]
        return jnp.sum(folded.T, axis=0, keepdims=True)

    a = acc[...]
    colx[0] = over_features(a * a + 1e-30)
    send_all(1, colx, True)

    for j in range(8):
        outgoing[j].wait_send()

    for p in range(CH):
        hop(z, p, True, own=True).wait_send()
        hop(z, p, False, own=True).wait_send()

    @pl.loop(1, 7)
    def _(s):
        bl, br = from_left(s), from_right(s)
        for p in range(CH):
            hop(bl, p, True).wait_send()
            hop(br, p, False).wait_send()

    for p in range(CH // 2):
        hop(bl, p, True).wait_send()
        hop(br, p + CH // 2, False).wait_send()

    whole(0, rowx, False).wait_recv()
    row_tot = jnp.sum(rowx[...], axis=0)
    nr = []
    lane = lax.broadcasted_iota(jnp.int32, (1, 128), 1)
    for m in range(2):
        v = 0.7 * rs_ref[m : m + 1, :] + 0.3 * (row_tot[:, m * FB : (m + 1) * FB] / FF)
        nr_ref[m : m + 1, :] = v
        nr.append(v)
    hid = lax.broadcasted_iota(jnp.int32, (W, FB), 0)
    u = acc[...] * jnp.where(hid < HB, lax.rsqrt(nr[0]), lax.rsqrt(nr[1]))
    ux[0, :, 0:W] = over_features(u * u)
    ux[0, :, W : W + 128] = jnp.where(
        lane == 0,
        jnp.sum(nr[0], axis=1, keepdims=True),
        jnp.sum(nr[1], axis=1, keepdims=True),
    )
    send_all(2, ux, True)
    acc[...] = u

    whole(1, colx, True).wait_recv()
    col_tot = jnp.sum(colx[...], axis=0)
    ncv = 0.7 * csv[...] + 0.3 * (col_tot / D)
    nc_ref[0:1, :] = ncv[:, :HB]
    nc_ref[1:2, :] = ncv[:, HB:]
    ccol = jnp.broadcast_to(lax.rsqrt(ncv), (128, W)).T
    acc[:, :128] = acc[:, :128] * ccol
    acc[:, 128:] = acc[:, 128:] * ccol
    ucopy = pltpu.make_async_copy(acc, upd_hbm, lsem.at[2])
    ucopy.start()

    whole(2, ux, True).wait_recv()
    u_tot = jnp.sum(ux[...], axis=0)
    share = u_tot[:, 0:W] / ncv
    first = lax.broadcasted_iota(jnp.int32, (1, W), 1) < HB
    s3x[0] = jnp.where(
        lane == 0,
        jnp.sum(jnp.where(first, share, 0.0), axis=1, keepdims=True),
        jnp.sum(jnp.where(first, 0.0, share), axis=1, keepdims=True),
    )
    send_all(3, s3x, False)
    level = u_tot[:, W : W + 128] / D
    whole(0, rowx, False).wait_send()
    whole(1, colx, True).wait_send()
    whole(2, ux, True).wait_send()
    ucopy.wait()
    whole(3, s3x, False).wait_recv()
    s_tot = jnp.sum(s3x[...], axis=0)
    urms = jnp.sqrt(level * (s_tot / (D * FF)))
    k_ref[...] = jnp.sqrt(level) / jnp.maximum(1.0, urms)
    whole(3, s3x, False).wait_send()


def finish(
    upd_hbm, nr_hbm, nc_hbm, k_hbm, out_hbm, nr_out, nc_out,
    buf, nr, nc, k, in_sem, out_sem,
):
    def piece(ref, i):
        return ref.at[pl.ds(i * QP, QP), :]

    copy = pltpu.make_async_copy
    ins = [copy(k_hbm, k, in_sem.at[QS])]
    ins += [copy(piece(upd_hbm, i), piece(buf, i), in_sem.at[i]) for i in range(QS)]
    small = [copy(nr_hbm, nr, in_sem.at[QS + 1]), copy(nc_hbm, nc, in_sem.at[QS + 2])]
    for cp in ins + small:
        cp.start()
    outs = [copy(piece(buf, i), piece(out_hbm, i), out_sem.at[i]) for i in range(QS)]
    outs += [copy(nr, nr_out, out_sem.at[QS]), copy(nc, nc_out, out_sem.at[QS + 1])]
    ins[0].wait()
    scale = k[...]
    for i in range(QS):
        ins[1 + i].wait()
        m = i // (QS // 2)
        rows = pl.ds(i * QP, QP)
        buf[rows, :] = buf[rows, :] * scale[:, m : m + 1]
        outs[i].start()
    for cp, out in zip(small, outs[QS:]):
        cp.wait()
        out.start()
    for out in outs:
        out.wait()


def shards(x_panel, grad_out, row_state, col_state):
    vmem = pl.BlockSpec(memory_space=pltpu.VMEM)
    anym = pl.BlockSpec(memory_space=pl.ANY)
    dma = pltpu.SemaphoreType.DMA
    grad_t = jnp.swapaxes(grad_out, 1, 2).reshape(W, TB)
    upd, new_rows, new_cols, k = pl.pallas_call(
        kernel,
        out_shape=(
            jax.ShapeDtypeStruct((W, FB), f32),
            jax.ShapeDtypeStruct((2, FB), f32),
            jax.ShapeDtypeStruct((2, HB), f32),
            jax.ShapeDtypeStruct((1, 128), f32),
        ),
        in_specs=[anym, anym, vmem, vmem],
        out_specs=(anym, vmem, vmem, vmem),
        scratch_shapes=[
            pltpu.VMEM((NZ, W, TB), jnp.bfloat16),
            pltpu.VMEM((NZ, TB, FB), jnp.bfloat16),
            pltpu.VMEM((W, FB), f32),
            pltpu.VMEM((1, W), f32),
            pltpu.VMEM((NC, 1, 2 * FB), f32),
            pltpu.VMEM((NZ, 1, W), f32),
            pltpu.VMEM((NZ, 1, W + 128), f32),
            pltpu.VMEM((NC, 1, 128), f32),
            dma((3,)),
            dma((NZ, CH)),
            dma((NZ, CH)),
            dma((NZ, CH)),
            dma((8,)),
            dma((8,)),
            dma((4,)),
            dma((4,)),
        ],
        compiler_params=pltpu.CompilerParams(
            collective_id=0, has_side_effects=True, vmem_limit_bytes=56 * 1024 * 1024
        ),
        cost_estimate=pl.CostEstimate(
            flops=2 * FB * W * 8192, bytes_accessed=3_000_000, transcendentals=0
        ),
    )(x_panel, grad_t, row_state, col_state)
    direction, new_rows, new_cols = pl.pallas_call(
        finish,
        out_shape=(
            jax.ShapeDtypeStruct((W, FB), f32),
            jax.ShapeDtypeStruct((2, FB), f32),
            jax.ShapeDtypeStruct((2, HB), f32),
        ),
        in_specs=[anym, anym, anym, anym],
        out_specs=(anym, anym, anym),
        scratch_shapes=[
            pltpu.VMEM((W, FB), f32),
            pltpu.VMEM((2, FB), f32),
            pltpu.VMEM((2, HB), f32),
            pltpu.VMEM((1, 128), f32),
            dma((QS + 3,)),
            dma((QS + 2,)),
        ],
    )(upd, new_rows, new_cols, k)
    direction = jnp.swapaxes(direction.reshape(2, HB, FB), 1, 2)
    return (direction, new_rows, new_cols)


def solution(mesh):
    return jax.shard_map(
        shards,
        mesh=mesh,
        in_specs=(P("col", "row"), P(None, "row", "col"), P(None, "row"), P(None, "col")),
        out_specs=(P(None, "row", "col"), P(None, "row"), P(None, "col")),
        check_vma=False,
    )
```
